32 devices in a mesh: dp: 4 (over z), ctx: 8 (over y, x, core).
Axes of the slice: x: 2, y: 2, z: 4, core: 2. Of those that a mesh axis runs over, the one named last changes fastest.
Arguments:
- hidden: bfloat16 [4, 2048, 8192], P('dp', 'ctx'), may hold values from -6 to 6
- queries: bfloat16 [4, 2048, 4096], P('dp', 'ctx')
- layout: int32 [4, 16], P('dp'), may hold values from 0 to 15, each once within a row
- boundary: int32 [4], P('dp'), may hold values from 1 to 2047
- key_matrix: bfloat16 [8192, 512], P(('dp', 'ctx')), may hold values from -0.0625 to 0.0625
- value_matrix: bfloat16 [8192, 512], P(('dp', 'ctx')), may hold values from -0.0625 to 0.0625
Outputs:
- attended: bfloat16 [4, 2048, 4096], P('dp', 'ctx')
The draws below stay inside these ranges and needn't reach their ends.
Inputs may be any that keep to these rules, and one draw needn't show every extreme that they name: Each row holds every block number of 0 to 15 once; local block b of ctx index c is layout[2 c + b].
All inputs are finite; a program needn't handle non-finite values.
Results may differ from the reference program's by a relative error of at most 0.011.
Values may be sent and summed in bfloat16 or wider, within the bound.
No kernel may reach another device: no remote copies, remote signals or barrier semaphores. Data moves between devices by JAX's collectives and lax.ppermute only.
A program may use at most 320 MiB of HBM per device.

```python
import jax
import jax.numpy as jnp
from jax import lax

MODEL_WIDTH = 8192
HQ = 32
KEY_VALUE_HEADS = 4
HEAD_WIDTH = 128
TOKENS_PER_SHARD = 256
QUERY_PER_KV = 8
HALF = 128
NBLK = 16
WINDOW_TOKENS = 2048
WINDOWS = 4


def draw_queries(key, part):
    first = jax.random.fold_in(key, 0)
    base = jnp.clip(jax.random.normal(first, (WINDOWS, WINDOW_TOKENS, HQ * HEAD_WIDTH), jnp.float32), -6.0, 6.0) * 2.5
    return base.astype(jnp.bfloat16)


def set_ends(entries, own_key, low, high):
    index_at = [jax.random.randint(jax.random.fold_in(own_key, axis), (), 0, length) for axis, length in enumerate(entries.shape)]
    widest = entries.shape.index(max(entries.shape))
    beside = index_at[:widest] + [(index_at[widest] + 1) % entries.shape[widest]] + index_at[widest + 1:]
    return entries.at[tuple(index_at)].set(low).at[tuple(beside)].set(high)


def block_scale(own_key, dims, shards, smallest, top_value):
    gain, own = 1.0, jax.random.fold_in(own_key, 6)
    for position, shards_of in shards:
        draws = jnp.exp(jax.random.uniform(jax.random.fold_in(own, position), (shards_of,), jnp.float32, smallest / len(shards), top_value / len(shards)))
        gain = gain * jnp.repeat(draws, dims[position] // shards_of).reshape([-1 if axis == position else 1 for axis in range(len(dims))])
    return gain


def centred(rng, dims, scale, most, cuts=(), held_as=jnp.bfloat16):
    values = jax.random.normal(rng, dims, jnp.float32) * scale
    if len(cuts) > 0:
        values = block_scale(rng, dims, cuts, -0.22, 0.18) * values
    return jnp.clip(values, min=-most, max=most).astype(held_as)


def setup_inputs(seed: int = 0) -> dict:
    arg_keys = jax.random.split(jax.random.key(seed), 7)
    return {
        "hidden": centred(arg_keys[0], (WINDOWS, WINDOW_TOKENS, MODEL_WIDTH), 1.0, 6.0, ((0, 4), (1, 8))),
        "queries": draw_queries(jax.random.fold_in(arg_keys[6], 71), 0),
        "layout": jax.vmap(lambda own: jax.random.permutation(own, NBLK))(jax.random.split(arg_keys[2], WINDOWS)).reshape((WINDOWS, NBLK)).astype(jnp.int32),
        "boundary": set_ends(jax.random.randint(arg_keys[3], (WINDOWS,), 1, WINDOW_TOKENS), jax.random.fold_in(arg_keys[3], 1), 1, WINDOW_TOKENS - 1).astype(jnp.int32),
        "key_matrix": centred(arg_keys[4], (MODEL_WIDTH, KEY_VALUE_HEADS * HEAD_WIDTH), MODEL_WIDTH ** -0.5, 0.0625, ((0, 32),)),
        "value_matrix": centred(arg_keys[5], (MODEL_WIDTH, KEY_VALUE_HEADS * HEAD_WIDTH), MODEL_WIDTH ** -0.5, 0.0625, ((0, 32),)),
    }


def reference(hidden, queries, layout, boundary, key_matrix, value_matrix):
    scale = HEAD_WIDTH ** -0.5

    def window(items):
        tokens, requested, order, start = items
        key_tensor = jnp.dot(tokens, key_matrix, preferred_element_type=jnp.float32).astype(jnp.bfloat16)
        value_tensor = jnp.dot(tokens, value_matrix, preferred_element_type=jnp.float32).astype(jnp.bfloat16)
        index = jnp.arange(WINDOW_TOKENS, dtype=jnp.int32)
        where_at = (order[index // HALF] * HALF + index % HALF).astype(jnp.int32)
        key_row_set = key_tensor.reshape(WINDOW_TOKENS, KEY_VALUE_HEADS, HEAD_WIDTH).astype(jnp.float32)
        value_row_set = value_tensor.reshape(WINDOW_TOKENS, KEY_VALUE_HEADS, HEAD_WIDTH).astype(jnp.float32)
        block_list = requested.reshape(WINDOW_TOKENS // TOKENS_PER_SHARD, TOKENS_PER_SHARD, KEY_VALUE_HEADS, QUERY_PER_KV, HEAD_WIDTH)
        block_pos = where_at.reshape(WINDOW_TOKENS // TOKENS_PER_SHARD, TOKENS_PER_SHARD)

        def block(parts):
            query_rows, query_pos = parts
            scores = jnp.einsum("qgha,kga->ghqk", query_rows.astype(jnp.float32), key_row_set) * scale
            allowed = (where_at[None, :] <= query_pos[:, None]) & ((where_at[None, :] >= start) | (query_pos[:, None] < start))
            scores = jnp.where(allowed, scores, -1e30)
            peak = jnp.max(scores, axis=-1)
            weights = jnp.where(allowed, jnp.exp(scores - peak[..., None]), 0.0)
            total = jnp.sum(weights, axis=-1)
            probs = lax.optimization_barrier(weights.astype(jnp.bfloat16))
            summed = jnp.einsum("ghqk,kga->ghqa", probs.astype(jnp.float32), value_row_set)
            result = summed / total[..., None]
            return result.transpose(2, 0, 1, 3).reshape(TOKENS_PER_SHARD, HQ * HEAD_WIDTH).astype(jnp.bfloat16)

        return lax.map(block, (block_list, block_pos)).reshape(WINDOW_TOKENS, HQ * HEAD_WIDTH)

    return lax.map(window, (hidden, queries, layout, boundary))
```

```python
import functools

import jax
import jax.numpy as jnp
from jax import lax
from jax.experimental import pallas as pl
from jax.experimental.pallas import tpu as pltpu
from jax.sharding import PartitionSpec as P

HEAD_WIDTH = 128
LOG2_E = 1.4426950408889634
VMEM_LIMIT = 48 * 2**20


def swapped(value, mask):
    size = lax.axis_size("ctx")
    return lax.ppermute(value, "ctx", [(i, i ^ mask) for i in range(size)])


def turned(value, by):
    size = lax.axis_size("dp")
    return lax.ppermute(value, "dp", [(i, (i + by) % size) for i in range(size)])


def doubled(value, masks):
    for mask in masks[:-1]:
        value = jnp.concatenate((value, swapped(value, mask)), axis=0)
    return [value, swapped(value, masks[-1])]


def xors(masks):
    found = [0]
    for mask in masks:
        found = found + [entry ^ mask for entry in found]
    return found


def project_kernel(count, starts, own_ref, other_ref, *refs):
    pieces, out_ref = refs[:-1], refs[-1]
    core = starts[0]
    rows = own_ref.shape[0]
    depth = sum(piece.shape[0] for piece in pieces) // count
    for source, place in ((own_ref, core), (other_ref, 1 - core)):
        total = jnp.zeros((rows, out_ref.shape[1]), jnp.float32)
        index = 0
        for piece in pieces:
            for part in range(piece.shape[0] // depth):
                first = pl.multiple_of(starts[1 + index] * depth, depth)
                total += jnp.dot(
                    source[:, pl.ds(first, depth)],
                    piece[part * depth : (part + 1) * depth, :],
                    preferred_element_type=jnp.float32,
                )
                index += 1
        out_ref[pl.ds(pl.multiple_of(place * rows, rows), rows), :] = total.astype(out_ref.dtype)


def project(starts, own, other, pieces):
    width = pieces[0].shape[1]
    rows = own.shape[0]
    vmem = pl.BlockSpec(memory_space=pltpu.VMEM)
    return pl.pallas_call(
        functools.partial(project_kernel, starts.shape[0] - 1),
        out_shape=jax.ShapeDtypeStruct((2 * rows, width), jnp.bfloat16),
        in_specs=[pl.BlockSpec(memory_space=pltpu.SMEM)] + [vmem] * (2 + len(pieces)),
        out_specs=vmem,
        compiler_params=pltpu.CompilerParams(vmem_limit_bytes=VMEM_LIMIT),
        cost_estimate=pl.CostEstimate(
            flops=4 * rows * own.shape[1] * width, bytes_accessed=6 * rows * own.shape[1], transcendentals=0
        ),
        name="project",
    )(starts, own, other, *pieces)


def attend_kernel(scale, starts, bias, queries, *refs):
    sides, (out_ref, key_rows, value_rows) = refs[:-3], refs[-3:]
    if len(sides) % 2:
        sides = sides[1:]
    held, sent = sides[: len(sides) // 2], sides[len(sides) // 2 :]
    is_keys = starts[0] == 0
    first = 0
    for one, two in zip(held, sent):
        span = pl.ds(first, one.shape[0])
        key_rows[span, :] = jnp.where(is_keys, one[...], two[...])
        value_rows[span, :HEAD_WIDTH] = jnp.where(is_keys, two[...], one[...])
        first += one.shape[0]
    value_rows[:, HEAD_WIDTH:] = jnp.ones((value_rows.shape[0], HEAD_WIDTH), jnp.bfloat16)
    step = 128
    for head in range(queries.shape[1] // HEAD_WIDTH):
        columns = slice(head * HEAD_WIDTH, (head + 1) * HEAD_WIDTH)
        for row in range(0, queries.shape[0], step):
            scores = lax.dot_general(
                queries[row : row + step, columns],
                key_rows[...],
                (((1,), (1,)), ((), ())),
                preferred_element_type=jnp.float32,
            )
            scores = scores * scale + bias[row : row + step, :]
            peak = jnp.max(scores, axis=1, keepdims=True)
            probs = jnp.exp2(scores - peak).astype(jnp.bfloat16)
            summed = jnp.dot(probs, value_rows[...], preferred_element_type=jnp.float32)
            out_ref[row : row + step, columns] = (summed[:, :HEAD_WIDTH] / summed[:, HEAD_WIDTH:]).astype(out_ref.dtype)


def attend(starts, bias, queries, sides, before, index, kv_heads):
    rows, width = queries.shape
    block = width // kv_heads
    count = bias.shape[1]
    vmem = pl.BlockSpec(memory_space=pltpu.VMEM)
    chosen = pl.BlockSpec((rows, block), lambda i: (0, index))
    in_specs = [pl.BlockSpec(memory_space=pltpu.SMEM), vmem, chosen]
    operands = [starts, bias, queries]
    aliases = {}
    if before is not None:
        aliases = {len(operands): 0}
        in_specs.append(pl.BlockSpec(memory_space=pl.ANY))
        operands.append(before)
    return pl.pallas_call(
        functools.partial(attend_kernel, HEAD_WIDTH**-0.5 * LOG2_E),
        grid=(1,),
        out_shape=jax.ShapeDtypeStruct((rows, width), jnp.bfloat16),
        in_specs=in_specs + [vmem] * len(sides),
        out_specs=chosen,
        input_output_aliases=aliases,
        scratch_shapes=[
            pltpu.VMEM((count, HEAD_WIDTH), jnp.bfloat16),
            pltpu.VMEM((count, 2 * HEAD_WIDTH), jnp.bfloat16),
        ],
        compiler_params=pltpu.CompilerParams(vmem_limit_bytes=VMEM_LIMIT),
        cost_estimate=pl.CostEstimate(
            flops=4 * rows * block * count, bytes_accessed=8 * rows * block, transcendentals=rows * count * block // HEAD_WIDTH
        ),
        name="attend",
    )(*operands, *sides)


def per_device(hidden, queries, layout, boundary, key_matrix, value_matrix):
    tokens, order, start_doc = hidden[0], layout[0], boundary[0]
    rows = tokens.shape[0]
    half = rows // 2
    kv_width = key_matrix.shape[1]
    kv_heads = kv_width // HEAD_WIDTH
    ctx_count, dp_count = lax.axis_size("ctx"), lax.axis_size("dp")
    here, window = lax.axis_index("ctx"), lax.axis_index("dp")
    core = here % 2
    chips = ctx_count // 2
    masks = [1 << bit for bit in range(1, ctx_count.bit_length() - 1)]

    is_keys = core == 0
    other_tokens = swapped(tokens, 1)
    mine = jnp.where(is_keys, key_matrix, value_matrix)
    theirs = swapped(jnp.where(is_keys, value_matrix, key_matrix), 1)
    matrix = jnp.concatenate((jnp.where(is_keys, mine, theirs), jnp.where(is_keys, theirs, mine)), axis=0)

    near, far = masks, masks[::-1]
    split = dp_count // 2
    places = [(by, xor) for xor in xors(near) for by in range(split)]
    places += [(by, xor) for xor in xors(far) for by in range(split, dp_count)]
    starts = jnp.stack(
        [core] + [((window - by) % dp_count) * chips + ((here ^ xor) // 2) for by, xor in places]
    ).astype(jnp.int32)

    sources = [here // 2 * 2 ^ xor for xor in xors(near)] + [here // 2 * 2 + 1 ^ xor for xor in xors(far)]
    block_ids = jnp.arange(order.shape[0], dtype=jnp.int32)

    def positions(devices):
        blocks = (jnp.stack(devices)[:, None] * 2 + jnp.arange(2)[None, :]).reshape(-1)
        looked = jnp.sum(jnp.where(blocks[:, None] == block_ids[None, :], order[None, :], 0), axis=1)
        return (looked[:, None] * half + jnp.arange(half, dtype=jnp.int32)[None, :]).reshape(-1)

    query_pos = positions([here])[:, None]
    key_pos = positions(sources)[None, :]
    allowed = (key_pos <= query_pos) & ((key_pos >= start_doc) | (query_pos < start_doc))
    bias = jnp.where(allowed, 0.0, -jnp.inf).astype(jnp.float32)

    result = None
    for index in range(kv_heads):
        piece = matrix[:, index * HEAD_WIDTH : (index + 1) * HEAD_WIDTH]
        parts = [piece] + [turned(piece, by) for by in range(1, dp_count)]
        pieces = doubled(jnp.concatenate(parts[:split], axis=0), near)
        pieces += doubled(jnp.concatenate(parts[split:], axis=0), far)
        made = project(starts, tokens, other_tokens, pieces)
        held = doubled(made[:rows], near) + doubled(made[rows:], far)
        sent = [swapped(side, 1) for side in held]
        result = attend(starts, bias, queries[0], held + sent, result, index, kv_heads)
    return result[None]


def solution(mesh):
    in_specs = (
        P("dp", "ctx", None),
        P("dp", "ctx", None),
        P("dp", None),
        P("dp"),
        P(("dp", "ctx"), None),
        P(("dp", "ctx"), None),
    )
    out_specs = P("dp", "ctx", None)
    return jax.shard_map(
        per_device, mesh=mesh, in_specs=in_specs, out_specs=out_specs, check_vma=False
    )
```

```python
import functools

import jax
import jax.numpy as jnp
from jax import lax
from jax.experimental import pallas as pl
from jax.experimental.pallas import tpu as pltpu
from jax.sharding import PartitionSpec as P

HEAD_WIDTH = 128
LOG2_E = 1.4426950408889634
ARRANGE_LIMIT = 12 * 2**20
PROJECT_LIMIT = 18 * 2**20
ATTEND_LIMIT = 14 * 2**20


def swapped(value, mask):
    size = lax.axis_size("ctx")
    return lax.ppermute(value, "ctx", [(i, i ^ mask) for i in range(size)])


def across(value, mask):
    size = lax.axis_size("dp")
    return lax.ppermute(value, "dp", [(i, i ^ mask) for i in range(size)])


def arrange_kernel(blocks, starts, own_ref, other_ref, out_ref, sems):
    core = starts[0]
    rows = own_ref.shape[0]
    depth = own_ref.shape[1] // blocks
    copies = []
    for source, place in ((own_ref, core), (other_ref, 1 - core)):
        for index in range(blocks):
            first = pl.multiple_of(starts[1 + index] * depth, depth)
            copies.append(
                pltpu.make_async_copy(
                    source.at[:, pl.ds(first, depth)],
                    out_ref.at[pl.ds(pl.multiple_of(place * rows, rows), rows), pl.ds(index * depth, depth)],
                    sems.at[len(copies)],
                )
            )
    for copy in copies:
        copy.start()
    for copy in copies:
        copy.wait()


def arrange(starts, own, other):
    blocks = starts.shape[0] - 1
    rows, columns = own.shape
    anywhere = pl.BlockSpec(memory_space=pl.ANY)
    return pl.pallas_call(
        functools.partial(arrange_kernel, blocks),
        out_shape=jax.ShapeDtypeStruct((2 * rows, columns), own.dtype),
        in_specs=[pl.BlockSpec(memory_space=pltpu.SMEM), anywhere, anywhere],
        out_specs=pl.BlockSpec(memory_space=pltpu.VMEM),
        scratch_shapes=[pltpu.SemaphoreType.DMA((2 * blocks,))],
        compiler_params=pltpu.CompilerParams(vmem_limit_bytes=ARRANGE_LIMIT),
        cost_estimate=pl.CostEstimate(flops=0, bytes_accessed=8 * rows * columns, transcendentals=0),
        name="arrange",
    )(starts, own, other)


def project_kernel(first, column, has_total, tokens, *refs):
    pieces, out_ref = refs[: -1 - has_total], refs[-1]
    width = out_ref.shape[1]
    total = refs[-2][:, column : column + width] if has_total else None
    for piece in pieces:
        depth = piece.shape[0]
        part = jnp.dot(tokens[:, first : first + depth], piece[...], preferred_element_type=jnp.float32)
        total = part if total is None else total + part
        first += depth
    out_ref[...] = total.astype(out_ref.dtype)


def project(tokens, first, pieces, total, column, dtype):
    rows, width = tokens.shape[0], pieces[0].shape[1]
    vmem = pl.BlockSpec(memory_space=pltpu.VMEM)
    depth = sum(piece.shape[0] for piece in pieces)
    totals = [] if total is None else [total]
    return pl.pallas_call(
        functools.partial(project_kernel, first, column, len(totals)),
        out_shape=jax.ShapeDtypeStruct((rows, width), dtype),
        in_specs=[vmem] * (1 + len(pieces) + len(totals)),
        out_specs=vmem,
        compiler_params=pltpu.CompilerParams(vmem_limit_bytes=PROJECT_LIMIT),
        cost_estimate=pl.CostEstimate(flops=2 * rows * depth * width, bytes_accessed=2 * rows * depth, transcendentals=0),
        name="project",
    )(tokens, *pieces, *totals)


def attend_kernel(scale, group, core, bias, queries, held, sent, *refs):
    out_ref, key_rows, value_rows = refs[-3:]
    is_keys = core[0] == 0
    key_rows[...] = jnp.where(is_keys, held[...], sent[...])
    value_rows[:, :HEAD_WIDTH] = jnp.where(is_keys, sent[...], held[...])
    value_rows[:, HEAD_WIDTH:] = jnp.ones((value_rows.shape[0], HEAD_WIDTH), jnp.bfloat16)
    step = 128
    for head in range(group):
        columns = slice(head * HEAD_WIDTH, (head + 1) * HEAD_WIDTH)
        for row in range(0, queries.shape[0], step):
            scores = lax.dot_general(
                queries[row : row + step, columns],
                key_rows[...],
                (((1,), (1,)), ((), ())),
                preferred_element_type=jnp.float32,
            )
            scores = scores * scale + bias[row : row + step, :]
            peak = jnp.max(scores, axis=1, keepdims=True)
            probs = jnp.exp2(scores - peak).astype(jnp.bfloat16)
            summed = jnp.dot(probs, value_rows[...], preferred_element_type=jnp.float32)
            out_ref[row : row + step, columns] = (summed[:, :HEAD_WIDTH] / summed[:, HEAD_WIDTH:]).astype(out_ref.dtype)


def attend(core, bias, queries, sides, before, first, head, kv_heads):
    rows, width = queries.shape
    block = width // kv_heads
    count = bias.shape[1]
    vmem = pl.BlockSpec(memory_space=pltpu.VMEM)
    chosen = pl.BlockSpec((rows, block), lambda i: (0, first + head))
    side = pl.BlockSpec((count, HEAD_WIDTH), lambda i: (0, head))
    in_specs = [pl.BlockSpec(memory_space=pltpu.SMEM), vmem, chosen, side, side]
    operands = [core, bias, queries, *sides]
    aliases = {}
    if before is not None:
        aliases = {len(operands): 0}
        in_specs.append(pl.BlockSpec(memory_space=pl.ANY))
        operands.append(before)
    return pl.pallas_call(
        functools.partial(attend_kernel, HEAD_WIDTH**-0.5 * LOG2_E, block // HEAD_WIDTH),
        grid=(1,),
        out_shape=jax.ShapeDtypeStruct((rows, width), jnp.bfloat16),
        in_specs=in_specs,
        out_specs=chosen,
        input_output_aliases=aliases,
        scratch_shapes=[
            pltpu.VMEM((count, HEAD_WIDTH), jnp.bfloat16),
            pltpu.VMEM((count, 2 * HEAD_WIDTH), jnp.bfloat16),
        ],
        compiler_params=pltpu.CompilerParams(vmem_limit_bytes=ATTEND_LIMIT),
        cost_estimate=pl.CostEstimate(
            flops=4 * rows * block * count,
            bytes_accessed=8 * rows * block,
            transcendentals=rows * count * block // HEAD_WIDTH,
        ),
        name="attend",
    )(*operands)


def per_device(hidden, queries, layout, boundary, key_matrix, value_matrix):
    tokens, order, start_doc = hidden[0], layout[0], boundary[0]
    rows_here = tokens.shape[0]
    half = rows_here // 2
    kv_width = key_matrix.shape[1]
    kv_heads = kv_width // HEAD_WIDTH
    ctx_count, dp_count = lax.axis_size("ctx"), lax.axis_size("dp")
    here, window = lax.axis_index("ctx"), lax.axis_index("dp")
    core = here % 2
    chips = ctx_count // 2
    masks = [1 << bit for bit in range(1, ctx_count.bit_length() - 1)]

    is_keys = core == 0
    mine = jnp.where(is_keys, key_matrix, value_matrix)
    theirs = swapped(jnp.where(is_keys, value_matrix, key_matrix), 1)
    matrix = jnp.concatenate((jnp.where(is_keys, mine, theirs), jnp.where(is_keys, theirs, mine)), axis=0)
    (other_tokens, _) = lax.optimization_barrier((tokens, theirs))
    other_tokens = swapped(other_tokens, 1)

    depth = matrix.shape[0] // 2
    far_masks = [1 << bit for bit in reversed(range(dp_count.bit_length() - 1))]

    def renamed(names, mask):
        return [(by, xor ^ mask, part) for by, xor, part in names]

    def all_names(names):
        for mask in masks[2:]:
            names = names + renamed(names, mask)
        low, high = masks[:2]
        return names + renamed(names, low) + renamed(names, high) + renamed(names, low ^ high)

    def nearby(rows):
        for mask in masks[2:]:
            rows = jnp.concatenate((rows, swapped(rows, mask)), axis=0)
        return [rows, swapped(rows, masks[0]), swapped(rows, masks[1])]

    def onward(pieces):
        rows, beside, above = pieces
        cut = rows.shape[0] // 2
        return [rows, beside, above, swapped(beside[:cut], masks[1]), swapped(above[cut:], masks[0])]

    def together(values, *others):
        joined = lax.optimization_barrier((*values, *others))
        return joined[: len(values)]

    plane = list(range(2, ctx_count, 2))

    def sent_round(made):
        return [made] + [swapped(made, xor) for xor in plane]

    def both_sides(parts):
        held = jnp.concatenate(parts, axis=0)
        return held, swapped(held, 1)

    sources = [(here // 2 * 2 ^ xor) + side for xor in [0] + plane for side in range(2)]
    block_ids = jnp.arange(order.shape[0], dtype=jnp.int32)

    def positions(devices):
        blocks = (jnp.stack(devices)[:, None] * 2 + jnp.arange(2)[None, :]).reshape(-1)
        looked = jnp.sum(jnp.where(blocks[:, None] == block_ids[None, :], order[None, :], 0), axis=1)
        return (looked[:, None] * half + jnp.arange(half, dtype=jnp.int32)[None, :]).reshape(-1)

    query_pos = positions([here])[:, None]
    key_pos = positions(sources)[None, :]
    allowed = (key_pos <= query_pos) & ((key_pos >= start_doc) | (query_pos < start_doc))
    bias = jnp.where(allowed, 0.0, -jnp.inf).astype(jnp.float32)

    cuts = [(0, 1), (1, kv_heads - 2), (kv_heads - 1, 1)]

    def wide(value, first, count):
        return value[:, first * HEAD_WIDTH : (first + count) * HEAD_WIDTH]

    names = all_names([(0, 0, part) for part in range(2)])
    column = [0]
    for mask in far_masks:
        column = column + [by ^ mask for by in column]
    names += all_names([(by, 0, part) for by in column[1:] for part in range(2)])
    starts = jnp.stack(
        [core] + [((window ^ by) * chips + ((here ^ xor) // 2)) * 2 + part for by, xor, part in names]
    ).astype(jnp.int32)
    ordered = depth % 128 == 0
    if ordered:
        arranged = arrange(starts, tokens, other_tokens)
    else:
        both = jnp.where(is_keys, 0, 1)
        arranged = jnp.stack((tokens, other_tokens))[jnp.stack((both, 1 - both))].reshape(2 * rows_here, -1)
        order_of = jnp.argsort(starts[1:])

    def project_cut(index, pieces):
        first, count = cuts[index]
        if ordered:
            return project(arranged, own_depth, pieces, own_total, first * HEAD_WIDTH, jnp.bfloat16)
        blocks = jnp.concatenate([wide(rows, first, count) for rows in own] + list(pieces), axis=0)
        blocks = jnp.take(blocks.reshape(-1, depth, count * HEAD_WIDTH), order_of, axis=0)
        return project(arranged, 0, [blocks.reshape(-1, count * HEAD_WIDTH)], None, 0, jnp.bfloat16)

    def attend_head(index, head, held, result):
        return attend(core[None], bias, queries[0], held, result, cuts[index][0], head, kv_heads)

    def columns_of(index):
        return wide(matrix, *cuts[index])

    def along(held, mask):
        return held + [across(held[0] if len(held) == 1 else jnp.concatenate(held, axis=0), mask)]

    def rest(held):
        return jnp.concatenate(held[1:], axis=0)

    own = nearby(matrix)
    column_a = along([columns_of(0)], far_masks[0])
    (start_b, *column_a) = together([columns_of(1), *column_a])
    for mask in far_masks[1:-1]:
        column_a = along(column_a, mask)
    column_a = along(column_a, far_masks[-1])
    column_b = along([start_b], far_masks[0])
    own = onward(own)
    own_depth = sum(rows.shape[0] for rows in own)
    (arranged, *column_a) = together([arranged, *column_a])
    near_a = nearby(rest(column_a))

    tick = list(together([*near_a, *own, *column_b, columns_of(2)]))
    near_a, own, column_b, column_c = tick[:3], tick[3:8], tick[8:-1], tick[-1:]
    all_a = onward(near_a)
    for mask in far_masks[1:]:
        column_b = along(column_b, mask)
    for mask in far_masks:
        column_c = along(column_c, mask)
    own_total = project(arranged, 0, own, None, 0, jnp.float32) if ordered else matrix

    tick = list(together([*all_a, own_total]))
    all_a, own_total = tick[:5], tick[5]
    parts_a = sent_round(project_cut(0, all_a))
    tick = list(together([*column_b, parts_a[0]]))
    column_b, parts_a[0] = tick[:-1], tick[-1]
    near_b = nearby(rest(column_b))
    result = attend_head(0, 0, both_sides(parts_a), None)

    tick = list(together([*near_b, *column_c, result]))
    near_b, column_c, result = tick[:3], tick[3:-1], tick[-1]
    all_b = onward(near_b)
    near_c = nearby(rest(column_c))

    tick = list(together([*all_b, *near_c]))
    all_b, near_c = tick[:5], tick[5:8]
    all_c = onward(near_c)
    parts_b = sent_round(project_cut(1, all_b))

    tick = list(together([*all_c, parts_b[0]]))
    all_c, parts_b[0] = tick[:5], tick[5]
    parts_c = sent_round(project_cut(2, all_c))
    side_b = both_sides(parts_b)
    side_b = together(side_b, parts_c[0])
    for head in range(cuts[1][1]):
        if head == cuts[1][1] - 1:
            (result, *parts_c) = together([result, *parts_c])
            side_c = both_sides(parts_c)
        result = attend_head(1, head, side_b, result)
    result = attend_head(2, 0, side_c, result)
    return result[None]


def solution(mesh):
    in_specs = (
        P("dp", "ctx", None),
        P("dp", "ctx", None),
        P("dp", None),
        P("dp"),
        P(("dp", "ctx"), None),
        P(("dp", "ctx"), None),
    )
    out_specs = P("dp", "ctx", None)
    return jax.shard_map(
        per_device, mesh=mesh, in_specs=in_specs, out_specs=out_specs, check_vma=False
    )
```

```python
import functools

import jax
import jax.numpy as jnp
from jax import lax
from jax.experimental import pallas as pl
from jax.experimental.pallas import tpu as pltpu
from jax.sharding import PartitionSpec as P

HEAD_WIDTH = 128
LOG2_E = 1.4426950408889634
ARRANGE_LIMIT = 12 * 2**20
PROJECT_LIMIT = 18 * 2**20
ATTEND_LIMIT = 14 * 2**20
REGROUP_LIMIT = 10 * 2**20


def swapped(value, mask):
    size = lax.axis_size("ctx")
    return lax.ppermute(value, "ctx", [(i, i ^ mask) for i in range(size)])


def across(value, mask):
    size = lax.axis_size("dp")
    return lax.ppermute(value, "dp", [(i, i ^ mask) for i in range(size)])


def arrange_kernel(blocks, starts, own_ref, other_ref, out_ref, sems):
    core = starts[0]
    rows = own_ref.shape[0]
    depth = own_ref.shape[1] // blocks
    copies = []
    for source, place in ((own_ref, core), (other_ref, 1 - core)):
        for index in range(blocks):
            first = pl.multiple_of(starts[1 + index] * depth, depth)
            copies.append(
                pltpu.make_async_copy(
                    source.at[:, pl.ds(first, depth)],
                    out_ref.at[pl.ds(pl.multiple_of(place * rows, rows), rows), pl.ds(index * depth, depth)],
                    sems.at[len(copies)],
                )
            )
    for copy in copies:
        copy.start()
    for copy in copies:
        copy.wait()


def arrange(starts, own, other):
    blocks = starts.shape[0] - 1
    rows, columns = own.shape
    anywhere = pl.BlockSpec(memory_space=pl.ANY)
    return pl.pallas_call(
        functools.partial(arrange_kernel, blocks),
        out_shape=jax.ShapeDtypeStruct((2 * rows, columns), own.dtype),
        in_specs=[pl.BlockSpec(memory_space=pltpu.SMEM), anywhere, anywhere],
        out_specs=pl.BlockSpec(memory_space=pltpu.VMEM),
        scratch_shapes=[pltpu.SemaphoreType.DMA((2 * blocks,))],
        compiler_params=pltpu.CompilerParams(vmem_limit_bytes=ARRANGE_LIMIT),
        cost_estimate=pl.CostEstimate(flops=0, bytes_accessed=8 * rows * columns, transcendentals=0),
        name="arrange",
    )(starts, own, other)


def project_kernel(runs, column, count, has_total, tokens, *refs):
    pieces, outs = refs[:count], refs[count + has_total :]
    width = sum(out.shape[1] for out in outs)
    total = refs[count][:, column : column + width] if has_total else None
    for piece, row, place, depth in runs:
        part = jnp.dot(
            tokens[:, place : place + depth], pieces[piece][row : row + depth, :], preferred_element_type=jnp.float32
        )
        total = part if total is None else total + part
    first = 0
    for out in outs:
        out[...] = total[:, first : first + out.shape[1]].astype(out.dtype)
        first += out.shape[1]


def project(tokens, runs, pieces, total, column, dtype, outs):
    rows, width = tokens.shape[0], pieces[0].shape[1]
    vmem = pl.BlockSpec(memory_space=pltpu.VMEM)
    depth = sum(run[3] for run in runs)
    totals = [] if total is None else [total]
    return pl.pallas_call(
        functools.partial(project_kernel, runs, column, len(pieces), len(totals)),
        out_shape=[jax.ShapeDtypeStruct((rows, width // outs), dtype)] * outs,
        in_specs=[vmem] * (1 + len(pieces) + len(totals)),
        out_specs=[vmem] * outs,
        compiler_params=pltpu.CompilerParams(vmem_limit_bytes=PROJECT_LIMIT),
        cost_estimate=pl.CostEstimate(flops=2 * rows * depth * width, bytes_accessed=2 * rows * depth, transcendentals=0),
        name="project",
    )(tokens, *pieces, *totals)


def attend_kernel(scale, group, query_first, side_first, flag, bias, queries, held, sent, *refs):
    out_ref, key_rows, value_rows, made, sems = refs[-5:]
    is_keys = flag[:1, :] > 0
    side = slice(side_first, side_first + HEAD_WIDTH)
    key_rows[...] = jnp.where(is_keys, held[:, side], sent[:, side])
    value_rows[:, :HEAD_WIDTH] = jnp.where(is_keys, sent[:, side], held[:, side])
    value_rows[:, HEAD_WIDTH:] = jnp.ones((value_rows.shape[0], HEAD_WIDTH), jnp.bfloat16)
    step = 128
    copies = []
    for head in range(group):
        columns = slice(query_first + head * HEAD_WIDTH, query_first + (head + 1) * HEAD_WIDTH)
        for row in range(0, queries.shape[0], step):
            scores = lax.dot_general(
                queries[row : row + step, columns],
                key_rows[...],
                (((1,), (1,)), ((), ())),
                preferred_element_type=jnp.float32,
            )
            scores = scores * scale + bias[row : row + step, :]
            peak = jnp.max(scores, axis=1, keepdims=True)
            probs = jnp.exp2(scores - peak).astype(jnp.bfloat16)
            summed = jnp.dot(probs, value_rows[...], preferred_element_type=jnp.float32)
            made[head, row : row + step, :] = (summed[:, :HEAD_WIDTH] / summed[:, HEAD_WIDTH:]).astype(made.dtype)
        copies.append(pltpu.make_async_copy(made.at[head], out_ref.at[:, columns], sems.at[head]))
        copies[-1].start()
    for copy in copies:
        copy.wait()


def attend(flag, bias, queries, sides, before, head, side_head, kv_heads):
    rows, width = queries.shape
    block = width // kv_heads
    group = block // HEAD_WIDTH
    count = bias.shape[1]
    vmem = pl.BlockSpec(memory_space=pltpu.VMEM)
    anywhere = pl.BlockSpec(memory_space=pl.ANY)
    operands = [flag, bias, queries, *sides]
    in_specs = [vmem] * 5
    aliases = {}
    if before is not None:
        aliases = {len(operands): 0}
        in_specs.append(anywhere)
        operands.append(before)
    return pl.pallas_call(
        functools.partial(attend_kernel, HEAD_WIDTH**-0.5 * LOG2_E, group, head * block, side_head * HEAD_WIDTH),
        out_shape=jax.ShapeDtypeStruct((rows, width), jnp.bfloat16),
        in_specs=in_specs,
        out_specs=anywhere,
        input_output_aliases=aliases,
        scratch_shapes=[
            pltpu.VMEM((count, HEAD_WIDTH), jnp.bfloat16),
            pltpu.VMEM((count, 2 * HEAD_WIDTH), jnp.bfloat16),
            pltpu.VMEM((group, rows, HEAD_WIDTH), jnp.bfloat16),
            pltpu.SemaphoreType.DMA((group,)),
        ],
        compiler_params=pltpu.CompilerParams(vmem_limit_bytes=ATTEND_LIMIT),
        cost_estimate=pl.CostEstimate(
            flops=4 * rows * block * count,
            bytes_accessed=8 * rows * block,
            transcendentals=rows * count * block // HEAD_WIDTH,
        ),
        name="attend",
    )(*operands)


def regroup_kernel(groups, count, *refs):
    for group, out_ref in zip(groups, refs[count:]):
        place = 0
        for index, row, rows, column in group:
            out_ref[place : place + rows, :] = refs[index][row : row + rows, column : column + out_ref.shape[1]]
            place += rows


def regroup(arrays, groups, widths):
    vmem = pl.BlockSpec(memory_space=pltpu.VMEM)
    return pl.pallas_call(
        functools.partial(regroup_kernel, groups, len(arrays)),
        out_shape=[
            jax.ShapeDtypeStruct((sum(part[2] for part in group), width), arrays[0].dtype)
            for group, width in zip(groups, widths)
        ],
        in_specs=[vmem] * len(arrays),
        out_specs=[vmem] * len(groups),
        compiler_params=pltpu.CompilerParams(vmem_limit_bytes=REGROUP_LIMIT),
        cost_estimate=pl.CostEstimate(flops=0, bytes_accessed=4 * sum(array.size for array in arrays), transcendentals=0),
        name="regroup",
    )(*arrays)


def assemble_kernel(flag, mine, theirs, out_ref):
    rows = mine.shape[0]
    is_first = flag[:1, :1] > 0
    out_ref[:rows, :] = jnp.where(is_first, mine[...], theirs[...])
    out_ref[rows:, :] = jnp.where(is_first, theirs[...], mine[...])


def assemble(flag, mine, theirs):
    rows, width = mine.shape
    vmem = pl.BlockSpec(memory_space=pltpu.VMEM)
    return pl.pallas_call(
        assemble_kernel,
        out_shape=jax.ShapeDtypeStruct((2 * rows, width), mine.dtype),
        in_specs=[vmem] * 3,
        out_specs=vmem,
        compiler_params=pltpu.CompilerParams(vmem_limit_bytes=REGROUP_LIMIT),
        name="assemble",
    )(flag, mine, theirs)


def per_device(hidden, queries, layout, boundary, key_matrix, value_matrix):
    tokens, order, start_doc = hidden[0], layout[0], boundary[0]
    rows_here = tokens.shape[0]
    half = rows_here // 2
    kv_width = key_matrix.shape[1]
    kv_heads = kv_width // HEAD_WIDTH
    ctx_count, dp_count = lax.axis_size("ctx"), lax.axis_size("dp")
    here, window = lax.axis_index("ctx"), lax.axis_index("dp")
    core = here % 2
    chips = ctx_count // 2
    masks = [1 << bit for bit in range(1, ctx_count.bit_length() - 1)]

    is_keys = core == 0
    mine = jnp.where(is_keys, key_matrix, value_matrix)
    theirs = swapped(jnp.where(is_keys, value_matrix, key_matrix), 1)
    flag = jnp.broadcast_to(is_keys.astype(jnp.float32), (8, HEAD_WIDTH))
    matrix = assemble(flag, mine, theirs)
    (other_tokens, _) = lax.optimization_barrier((tokens, theirs))
    other_tokens = swapped(other_tokens, 1)

    depth = matrix.shape[0] // 2
    far_masks = [1 << bit for bit in reversed(range(dp_count.bit_length() - 1))]

    def by_plane(piece, mask):
        return swapped(piece[0], mask), [(by, xor ^ mask, part) for by, xor, part in piece[1]]

    def by_column(piece, mask):
        return across(piece[0], mask), [(by ^ mask, xor, part) for by, xor, part in piece[1]]

    def view(piece, first_name=0, count=None, start=0, columns=None):
        array, names = piece
        names = names[first_name : None if count is None else first_name + count]
        return array, first_name * depth, names, start, array.shape[1] - start if columns is None else columns

    def first(piece, **columns):
        return view(piece, 0, len(piece[1]) // 2, **columns)

    def second(piece, **columns):
        return view(piece, len(piece[1]) // 2, **columns)

    def joined(*lists):
        arrays, groups = [], []
        for views in lists:
            group = []
            for array, row, names, start, _ in views:
                index = [k for k, known in enumerate(arrays) if known is array]
                if not index:
                    arrays.append(array)
                    index = [len(arrays) - 1]
                group.append((index[0], row, len(names) * depth, start))
            groups.append(tuple(group))
        made = regroup(arrays, tuple(groups), [views[0][4] for views in lists])
        return [(rows, sum([one[2] for one in views], [])) for rows, views in zip(made, lists)]

    def nearby(piece):
        for mask in masks[2:]:
            (piece,) = joined([view(piece), view(by_plane(piece, mask))])
        return [piece, by_plane(piece, masks[0]), by_plane(piece, masks[1])]

    def onward(pieces):
        low, high = joined([first(pieces[1])], [second(pieces[2])])
        return pieces + [by_plane(low, masks[1]), by_plane(high, masks[0])]

    def along(held, mask):
        whole = held[0] if len(held) == 1 else joined([view(piece) for piece in held])[0]
        return held + [by_column(whole, mask)]

    def tied(values, *others):
        arrays = [value[0] if isinstance(value, tuple) else value for value in values]
        after = lax.optimization_barrier((*arrays, *others))
        return [(array, value[1]) if isinstance(value, tuple) else array for array, value in zip(after, values)]

    plane = list(range(2, ctx_count, 2))

    def sent_round(made):
        return [made] + [swapped(made, xor) for xor in plane]

    def both_sides(parts):
        rows, width = parts[0].shape
        (held,) = regroup(parts, (tuple((index, 0, rows, 0) for index in range(len(parts))),), [width])
        return held, swapped(held, 1)

    sources = [(here // 2 * 2 ^ xor) + side for xor in [0] + plane for side in range(2)]
    block_ids = jnp.arange(order.shape[0], dtype=jnp.int32)

    def positions(devices):
        blocks = (jnp.stack(devices)[:, None] * 2 + jnp.arange(2)[None, :]).reshape(-1)
        looked = jnp.sum(jnp.where(blocks[:, None] == block_ids[None, :], order[None, :], 0), axis=1)
        return (looked[:, None] * half + jnp.arange(half, dtype=jnp.int32)[None, :]).reshape(-1)

    query_pos = positions([here])[:, None]
    key_pos = positions(sources)[None, :]
    allowed = (key_pos <= query_pos) & ((key_pos >= start_doc) | (query_pos < start_doc))
    bias = jnp.where(allowed, 0.0, -jnp.inf).astype(jnp.float32)

    cuts = [(0, 1), (1, kv_heads - 2), (kv_heads - 1, 1)]

    def cut(index):
        start, count = cuts[index]
        return {"start": start * HEAD_WIDTH, "columns": count * HEAD_WIDTH}

    column = [0]
    for mask in far_masks:
        column = column + [by ^ mask for by in column]
    plane_xors = [0, masks[0], masks[1], masks[0] ^ masks[1]]
    for mask in masks[2:]:
        plane_xors = plane_xors + [xor ^ mask for xor in plane_xors]
    own_order = [(0, xor, part) for xor in plane_xors for part in range(2)]
    order_of = own_order + [(by, xor, part) for xor in plane_xors for part in range(2) for by in column[1:]]
    starts = [((window ^ by) * chips + ((here ^ xor) // 2)) * 2 + part for by, xor, part in order_of]
    ordered = depth % 128 == 0
    if ordered:
        arranged = arrange(jnp.stack([core, *starts]).astype(jnp.int32), tokens, other_tokens)
    else:
        both = jnp.where(is_keys, 0, 1)
        arranged = jnp.stack((tokens, other_tokens))[jnp.stack((both, 1 - both))].reshape(2 * rows_here, -1)
        arranged = jnp.take(arranged.reshape(2 * rows_here, -1, depth), jnp.stack(starts), axis=1)
        arranged = arranged.reshape(2 * rows_here, -1)

    def project_pieces(pieces, total, start, dtype):
        runs = []
        for index, (_, names) in enumerate(pieces):
            for block, name in enumerate(names):
                row, place = block * depth, order_of.index(name) * depth
                if runs and runs[-1][0] == index and runs[-1][2] + runs[-1][3] == place:
                    runs[-1] = (*runs[-1][:3], runs[-1][3] + depth)
                else:
                    runs.append((index, row, place, depth))
        return project(arranged, tuple(runs), [rows for rows, _ in pieces], total, start * HEAD_WIDTH, dtype, 1)

    def project_cut(index, pieces):
        return project_pieces(pieces, own_total, cuts[index][0], jnp.bfloat16)

    def attend_head(head, held, result, side_head=0):
        return attend(flag, bias, queries[0], held, result, head, side_head, kv_heads)

    mine_rows = (matrix, [(0, 0, 0), (0, 0, 1)])
    own = nearby(mine_rows)
    column_a = along(joined([view(mine_rows, **cut(0))]), far_masks[0])
    for mask in far_masks[1:]:
        column_a = along(column_a, mask)

    def halves(index):
        low = [first(own[0], **cut(index)), first(own[1], **cut(index))]
        high = [second(own[0], **cut(index)), second(own[2], **cut(index))]
        return low + high

    (start_b,) = tied(joined([view(mine_rows, **cut(1))]), column_a[-1][0])
    column_b = along([start_b], far_masks[0])
    all_own = onward(own)

    def sorted_views(held, places):
        size = len(held[0][1])
        part = size // places
        views = [[] for _ in range(places)]
        for piece in held[1:]:
            for block in range(0, len(piece[1]), size):
                for place in range(places):
                    views[place].append(view(piece, block + place * part, part))
        return views

    (rest_a,) = joined(sum(sorted_views(column_a, 2), []))
    near_a = nearby(rest_a)

    def last_exchange(held):
        views = sorted_views(held, 4)
        low, high = joined(views[0] + views[1], views[2] + views[3])
        return [low, high, by_plane(low, masks[1]), by_plane(high, masks[0])]

    tick = tied([arranged, *near_a, *all_own, *column_b])
    arranged, near_a, all_own, column_b = tick[0], tick[1:4], tick[4:9], tick[9:]
    all_a = onward(near_a)
    for mask in far_masks[1:]:
        column_b = along(column_b, mask)
    (own_total,) = project_pieces(all_own, None, 0, jnp.float32)

    tick = tied([own_total, *all_a])
    own_total, all_a = tick[0], tick[1:]
    (made_a,) = project_cut(0, all_a)
    parts_a = sent_round(made_a)
    (rest_b,) = joined(sum(sorted_views(column_b, 2), []))
    near_b = nearby(rest_b)
    (start_c,) = tied(joined(halves(2)), column_b[-1][0])
    column_c = [start_c]
    for mask in far_masks:
        column_c = along(column_c, mask)
    result = attend_head(0, both_sides(parts_a), None)

    tick = tied([result, *near_b, *column_c])
    result, near_b, column_c = tick[0], tick[1:4], tick[4:]
    all_b = onward(near_b)
    all_c = last_exchange(column_c)
    (part_b,) = project_pieces(all_b[:3], own_total, cuts[1][0], jnp.float32)
    part_b, *last_b = tied([part_b, *all_b[3:]])
    (made_b,) = project_pieces(last_b, part_b, 0, jnp.bfloat16)

    parts_b = sent_round(made_b)
    (part_c,) = project_pieces(all_c[:2], own_total, cuts[2][0], jnp.float32)
    part_c, parts_b[0], *last_c = tied([part_c, parts_b[0], *all_c[2:]])
    (made_c,) = project_pieces(last_c, part_c, 0, jnp.bfloat16)
    parts_c = sent_round(made_c)
    tick = tied([*parts_b, parts_c[0]])
    parts_b, parts_c[0] = tick[:-1], tick[-1]
    side_b = both_sides(parts_b)
    count = cuts[1][1]
    for head in range(count):
        if head == count - 1:
            result, *parts_c = tied([result, *parts_c])
            side_c = both_sides(parts_c)
        result = attend_head(1 + head, side_b, result, head)
    result = attend_head(kv_heads - 1, side_c, result)
    return result[None]


def solution(mesh):
    in_specs = (
        P("dp", "ctx", None),
        P("dp", "ctx", None),
        P("dp", None),
        P("dp"),
        P(("dp", "ctx"), None),
        P(("dp", "ctx"), None),
    )
    out_specs = P("dp", "ctx", None)
    return jax.shard_map(
        per_device, mesh=mesh, in_specs=in_specs, out_specs=out_specs, check_vma=False
    )
```

```python
import functools

import jax
import jax.numpy as jnp
from jax import lax
from jax.experimental import pallas as pl
from jax.experimental.pallas import tpu as pltpu
from jax.sharding import PartitionSpec as P

HEAD_WIDTH = 128
LOG2_E = 1.4426950408889634
ARRANGE_LIMIT = 12 * 2**20
PROJECT_LIMIT = 18 * 2**20
ATTEND_LIMIT = 14 * 2**20
REGROUP_LIMIT = 10 * 2**20


def swapped(value, mask):
    size = lax.axis_size("ctx")
    return lax.ppermute(value, "ctx", [(i, i ^ mask) for i in range(size)])


def across(value, mask):
    size = lax.axis_size("dp")
    return lax.ppermute(value, "dp", [(i, i ^ mask) for i in range(size)])


def arrange_kernel(blocks, starts, own_ref, other_ref, out_ref, sems):
    core = starts[0]
    rows = own_ref.shape[0]
    depth = own_ref.shape[1] // blocks
    copies = []
    for source, place in ((own_ref, core), (other_ref, 1 - core)):
        for index in range(blocks):
            first = pl.multiple_of(starts[1 + index] * depth, depth)
            copies.append(
                pltpu.make_async_copy(
                    source.at[:, pl.ds(first, depth)],
                    out_ref.at[pl.ds(pl.multiple_of(place * rows, rows), rows), pl.ds(index * depth, depth)],
                    sems.at[len(copies)],
                )
            )
    for copy in copies:
        copy.start()
    for copy in copies:
        copy.wait()


def arrange(starts, own, other):
    blocks = starts.shape[0] - 1
    rows, columns = own.shape
    anywhere = pl.BlockSpec(memory_space=pl.ANY)
    return pl.pallas_call(
        functools.partial(arrange_kernel, blocks),
        out_shape=jax.ShapeDtypeStruct((2 * rows, columns), own.dtype),
        in_specs=[pl.BlockSpec(memory_space=pltpu.SMEM), anywhere, anywhere],
        out_specs=pl.BlockSpec(memory_space=pltpu.VMEM),
        scratch_shapes=[pltpu.SemaphoreType.DMA((2 * blocks,))],
        compiler_params=pltpu.CompilerParams(vmem_limit_bytes=ARRANGE_LIMIT),
        cost_estimate=pl.CostEstimate(flops=0, bytes_accessed=8 * rows * columns, transcendentals=0),
        name="arrange",
    )(starts, own, other)


def project_kernel(runs, column, count, has_total, tokens, *refs):
    pieces, outs = refs[:count], refs[count + has_total :]
    width = sum(out.shape[1] for out in outs)
    total = refs[count][:, column : column + width] if has_total else None
    for piece, row, place, depth in runs:
        part = jnp.dot(
            tokens[:, place : place + depth], pieces[piece][row : row + depth, :], preferred_element_type=jnp.float32
        )
        total = part if total is None else total + part
    first = 0
    for out in outs:
        out[...] = total[:, first : first + out.shape[1]].astype(out.dtype)
        first += out.shape[1]


def project(tokens, runs, pieces, total, column, dtype, outs):
    rows, width = tokens.shape[0], pieces[0].shape[1]
    vmem = pl.BlockSpec(memory_space=pltpu.VMEM)
    depth = sum(run[3] for run in runs)
    totals = [] if total is None else [total]
    return pl.pallas_call(
        functools.partial(project_kernel, runs, column, len(pieces), len(totals)),
        out_shape=[jax.ShapeDtypeStruct((rows, width // outs), dtype)] * outs,
        in_specs=[vmem] * (1 + len(pieces) + len(totals)),
        out_specs=[vmem] * outs,
        compiler_params=pltpu.CompilerParams(vmem_limit_bytes=PROJECT_LIMIT),
        cost_estimate=pl.CostEstimate(flops=2 * rows * depth * width, bytes_accessed=2 * rows * depth, transcendentals=0),
        name="project",
    )(tokens, *pieces, *totals)


def attend_kernel(scale, group, query_first, side_first, flag, bias, queries, held, sent, *refs):
    out_ref, key_rows, value_rows, made, sems = refs[-5:]
    is_keys = flag[:1, :] > 0
    side = slice(side_first, side_first + HEAD_WIDTH)
    key_rows[...] = jnp.where(is_keys, held[:, side], sent[:, side])
    value_rows[:, :HEAD_WIDTH] = jnp.where(is_keys, sent[:, side], held[:, side])
    value_rows[:, HEAD_WIDTH:] = jnp.ones((value_rows.shape[0], HEAD_WIDTH), jnp.bfloat16)
    step = 128
    copies = []
    for head in range(group):
        columns = slice(query_first + head * HEAD_WIDTH, query_first + (head + 1) * HEAD_WIDTH)
        for row in range(0, queries.shape[0], step):
            scores = lax.dot_general(
                queries[row : row + step, columns],
                key_rows[...],
                (((1,), (1,)), ((), ())),
                preferred_element_type=jnp.float32,
            )
            scores = scores * scale + bias[row : row + step, :]
            peak = jnp.max(scores, axis=1, keepdims=True)
            probs = jnp.exp2(scores - peak).astype(jnp.bfloat16)
            summed = jnp.dot(probs, value_rows[...], preferred_element_type=jnp.float32)
            made[head, row : row + step, :] = (summed[:, :HEAD_WIDTH] / summed[:, HEAD_WIDTH:]).astype(made.dtype)
        copies.append(pltpu.make_async_copy(made.at[head], out_ref.at[:, columns], sems.at[head]))
        copies[-1].start()
    for copy in copies:
        copy.wait()


def attend(flag, bias, queries, sides, before, head, side_head, kv_heads):
    rows, width = queries.shape
    block = width // kv_heads
    group = block // HEAD_WIDTH
    count = bias.shape[1]
    vmem = pl.BlockSpec(memory_space=pltpu.VMEM)
    anywhere = pl.BlockSpec(memory_space=pl.ANY)
    operands = [flag, bias, queries, *sides]
    in_specs = [vmem] * 5
    aliases = {}
    if before is not None:
        aliases = {len(operands): 0}
        in_specs.append(anywhere)
        operands.append(before)
    return pl.pallas_call(
        functools.partial(attend_kernel, HEAD_WIDTH**-0.5 * LOG2_E, group, head * block, side_head * HEAD_WIDTH),
        out_shape=jax.ShapeDtypeStruct((rows, width), jnp.bfloat16),
        in_specs=in_specs,
        out_specs=anywhere,
        input_output_aliases=aliases,
        scratch_shapes=[
            pltpu.VMEM((count, HEAD_WIDTH), jnp.bfloat16),
            pltpu.VMEM((count, 2 * HEAD_WIDTH), jnp.bfloat16),
            pltpu.VMEM((group, rows, HEAD_WIDTH), jnp.bfloat16),
            pltpu.SemaphoreType.DMA((group,)),
        ],
        compiler_params=pltpu.CompilerParams(vmem_limit_bytes=ATTEND_LIMIT),
        cost_estimate=pl.CostEstimate(
            flops=4 * rows * block * count,
            bytes_accessed=8 * rows * block,
            transcendentals=rows * count * block // HEAD_WIDTH,
        ),
        name="attend",
    )(*operands)


def regroup_kernel(groups, count, *refs):
    for group, out_ref in zip(groups, refs[count:]):
        place = 0
        for index, row, rows, column in group:
            out_ref[place : place + rows, :] = refs[index][row : row + rows, column : column + out_ref.shape[1]]
            place += rows


def regroup(arrays, groups, widths):
    vmem = pl.BlockSpec(memory_space=pltpu.VMEM)
    return pl.pallas_call(
        functools.partial(regroup_kernel, groups, len(arrays)),
        out_shape=[
            jax.ShapeDtypeStruct((sum(part[2] for part in group), width), arrays[0].dtype)
            for group, width in zip(groups, widths)
        ],
        in_specs=[vmem] * len(arrays),
        out_specs=[vmem] * len(groups),
        compiler_params=pltpu.CompilerParams(vmem_limit_bytes=REGROUP_LIMIT),
        cost_estimate=pl.CostEstimate(flops=0, bytes_accessed=4 * sum(array.size for array in arrays), transcendentals=0),
        name="regroup",
    )(*arrays)


def assemble_kernel(flag, mine, theirs, out_ref):
    rows = mine.shape[0]
    is_first = flag[:1, :1] > 0
    out_ref[:rows, :] = jnp.where(is_first, mine[...], theirs[...])
    out_ref[rows:, :] = jnp.where(is_first, theirs[...], mine[...])


def assemble(flag, mine, theirs):
    rows, width = mine.shape
    vmem = pl.BlockSpec(memory_space=pltpu.VMEM)
    return pl.pallas_call(
        assemble_kernel,
        out_shape=jax.ShapeDtypeStruct((2 * rows, width), mine.dtype),
        in_specs=[vmem] * 3,
        out_specs=vmem,
        compiler_params=pltpu.CompilerParams(vmem_limit_bytes=REGROUP_LIMIT),
        name="assemble",
    )(flag, mine, theirs)


def per_device(hidden, queries, layout, boundary, key_matrix, value_matrix):
    tokens, order, start_doc = hidden[0], layout[0], boundary[0]
    rows_here = tokens.shape[0]
    half = rows_here // 2
    kv_width = key_matrix.shape[1]
    kv_heads = kv_width // HEAD_WIDTH
    ctx_count, dp_count = lax.axis_size("ctx"), lax.axis_size("dp")
    here, window = lax.axis_index("ctx"), lax.axis_index("dp")
    core = here % 2
    chips = ctx_count // 2
    masks = [1 << bit for bit in range(1, ctx_count.bit_length() - 1)]

    is_keys = core == 0
    mine = jnp.where(is_keys, key_matrix, value_matrix)
    theirs = swapped(jnp.where(is_keys, value_matrix, key_matrix), 1)
    flag = jnp.broadcast_to(is_keys.astype(jnp.float32), (8, HEAD_WIDTH))
    matrix = assemble(flag, mine, theirs)
    (other_tokens, _) = lax.optimization_barrier((tokens, theirs))
    other_tokens = swapped(other_tokens, 1)

    depth = matrix.shape[0] // 2
    far_masks = [1 << bit for bit in reversed(range(dp_count.bit_length() - 1))]

    def by_plane(piece, mask):
        return swapped(piece[0], mask), [(by, xor ^ mask, part) for by, xor, part in piece[1]]

    def by_column(piece, mask):
        return across(piece[0], mask), [(by ^ mask, xor, part) for by, xor, part in piece[1]]

    def view(piece, first_name=0, count=None, start=0, columns=None):
        array, names = piece
        names = names[first_name : None if count is None else first_name + count]
        return array, first_name * depth, names, start, array.shape[1] - start if columns is None else columns

    def first(piece, **columns):
        return view(piece, 0, len(piece[1]) // 2, **columns)

    def second(piece, **columns):
        return view(piece, len(piece[1]) // 2, **columns)

    def joined(*lists):
        arrays, groups = [], []
        for views in lists:
            group = []
            for array, row, names, start, _ in views:
                index = [k for k, known in enumerate(arrays) if known is array]
                if not index:
                    arrays.append(array)
                    index = [len(arrays) - 1]
                group.append((index[0], row, len(names) * depth, start))
            groups.append(tuple(group))
        made = regroup(arrays, tuple(groups), [views[0][4] for views in lists])
        return [(rows, sum([one[2] for one in views], [])) for rows, views in zip(made, lists)]

    def nearby(piece):
        for mask in masks[2:]:
            (piece,) = joined([view(piece), view(by_plane(piece, mask))])
        return [piece, by_plane(piece, masks[0]), by_plane(piece, masks[1])]

    def onward(pieces):
        low, high = joined([first(pieces[1])], [second(pieces[2])])
        return pieces + [by_plane(low, masks[1]), by_plane(high, masks[0])]

    def along(held, mask):
        whole = held[0] if len(held) == 1 else joined([view(piece) for piece in held])[0]
        return held + [by_column(whole, mask)]

    def tied(values, *others):
        arrays = [value[0] if isinstance(value, tuple) else value for value in values]
        after = lax.optimization_barrier((*arrays, *others))
        return [(array, value[1]) if isinstance(value, tuple) else array for array, value in zip(after, values)]

    plane = list(range(2, ctx_count, 2))

    def sent_round(made):
        return [made] + [swapped(made, xor) for xor in plane]

    def both_sides(parts):
        rows, width = parts[0].shape
        (held,) = regroup(parts, (tuple((index, 0, rows, 0) for index in range(len(parts))),), [width])
        return held, swapped(held, 1)

    sources = [(here // 2 * 2 ^ xor) + side for xor in [0] + plane for side in range(2)]
    block_ids = jnp.arange(order.shape[0], dtype=jnp.int32)

    def positions(devices):
        blocks = (jnp.stack(devices)[:, None] * 2 + jnp.arange(2)[None, :]).reshape(-1)
        looked = jnp.sum(jnp.where(blocks[:, None] == block_ids[None, :], order[None, :], 0), axis=1)
        return (looked[:, None] * half + jnp.arange(half, dtype=jnp.int32)[None, :]).reshape(-1)

    query_pos = positions([here])[:, None]
    key_pos = positions(sources)[None, :]
    allowed = (key_pos <= query_pos) & ((key_pos >= start_doc) | (query_pos < start_doc))
    bias = jnp.where(allowed, 0.0, -jnp.inf).astype(jnp.float32)

    cuts = [(0, 1), (1, 2), (3, 1)]

    def cut(index):
        start, count = cuts[index]
        return {"start": start * HEAD_WIDTH, "columns": count * HEAD_WIDTH}

    column = [0]
    for mask in far_masks:
        column = column + [by ^ mask for by in column]
    plane_xors = [0, masks[0], masks[1], masks[0] ^ masks[1]]
    for mask in masks[2:]:
        plane_xors = plane_xors + [xor ^ mask for xor in plane_xors]
    own_order = [(0, xor, part) for xor in plane_xors for part in range(2)]
    order_of = own_order + [(by, xor, part) for xor in plane_xors for part in range(2) for by in column[1:]]
    starts = [((window ^ by) * chips + ((here ^ xor) // 2)) * 2 + part for by, xor, part in order_of]
    ordered = depth % 128 == 0
    if ordered:
        arranged = arrange(jnp.stack([core, *starts]).astype(jnp.int32), tokens, other_tokens)
    else:
        both = jnp.where(is_keys, 0, 1)
        arranged = jnp.stack((tokens, other_tokens))[jnp.stack((both, 1 - both))].reshape(2 * rows_here, -1)
        arranged = jnp.take(arranged.reshape(2 * rows_here, -1, depth), jnp.stack(starts), axis=1)
        arranged = arranged.reshape(2 * rows_here, -1)

    def project_pieces(pieces, total, start, dtype):
        runs = []
        for index, (_, names) in enumerate(pieces):
            for block, name in enumerate(names):
                row, place = block * depth, order_of.index(name) * depth
                if runs and runs[-1][0] == index and runs[-1][2] + runs[-1][3] == place:
                    runs[-1] = (*runs[-1][:3], runs[-1][3] + depth)
                else:
                    runs.append((index, row, place, depth))
        return project(arranged, tuple(runs), [rows for rows, _ in pieces], total, start * HEAD_WIDTH, dtype, 1)

    def project_cut(index, pieces):
        return project_pieces(pieces, own_total, cuts[index][0], jnp.bfloat16)

    def attend_head(head, held, result, side_head=0):
        return attend(flag, bias, queries[0], held, result, head, side_head, kv_heads)

    mine_rows = (matrix, [(0, 0, 0), (0, 0, 1)])
    own = nearby(mine_rows)
    column_a = along(joined([view(mine_rows, **cut(0))]), far_masks[0])
    for mask in far_masks[1:]:
        column_a = along(column_a, mask)

    def halves(index):
        low = [first(own[0], **cut(index)), first(own[1], **cut(index))]
        high = [second(own[0], **cut(index)), second(own[2], **cut(index))]
        return low + high

    (start_b,) = tied(joined([view(mine_rows, **cut(1))]), column_a[-1][0])
    column_b = along([start_b], far_masks[0])
    all_own = onward(own)

    def sorted_views(held, places, **columns):
        size = len(held[0][1])
        part = size // places
        views = [[] for _ in range(places)]
        for piece in held[1:]:
            for block in range(0, len(piece[1]), size):
                for place in range(places):
                    views[place].append(view(piece, block + place * part, part, **columns))
        return views

    (rest_a,) = joined(sum(sorted_views(column_a, 2), []))
    near_a = nearby(rest_a)

    def last_exchange(held):
        views = sorted_views(held, 4)
        low, high = joined(views[0] + views[1], views[2] + views[3])
        return [low, high, by_plane(low, masks[1]), by_plane(high, masks[0])]

    tick = tied([arranged, *near_a, *all_own, *column_b])
    arranged, near_a, all_own, column_b = tick[0], tick[1:4], tick[4:9], tick[9:]
    all_a = onward(near_a)
    for mask in far_masks[1:]:
        column_b = along(column_b, mask)
    (own_total,) = project_pieces(all_own, None, 0, jnp.float32)

    tick = tied([own_total, *all_a])
    own_total, all_a = tick[0], tick[1:]
    (made_a,) = project_cut(0, all_a)
    parts_a = sent_round(made_a)
    rest_b, rest_c = joined(
        *[sum(sorted_views(column_b, 2, start=first * HEAD_WIDTH, columns=HEAD_WIDTH), []) for first in range(2)]
    )
    near_b = nearby(rest_b)
    (made_a,) = project_cut(0, all_a)
    parts_a = sent_round(made_a)
    (start_d, rest_c, *parts_a) = tied([*joined(halves(2)), rest_c, *parts_a])
    near_c = nearby(rest_c)
    column_d = along([start_d], far_masks[0])
    result = attend_head(0, both_sides(parts_a), None)

    tick = tied([result, *near_b])
    result, near_b = tick[0], tick[1:]
    all_b = onward(near_b)
    (part_b,) = project_pieces(all_b[:3], own_total, 1, jnp.float32)
    part_b, *column_d = tied([part_b, *column_d])
    for mask in far_masks[1:]:
        column_d = along(column_d, mask)

    tick = tied([part_b, *all_b[3:], *near_c])
    part_b, last_b, near_c = tick[0], tick[1:3], tick[3:]
    all_c = onward(near_c)
    (made_b,) = project_pieces(last_b, part_b, 0, jnp.bfloat16)
    parts_b = sent_round(made_b)
    (part_c,) = project_pieces(all_c[:3], own_total, 2, jnp.float32)

    tick = tied([part_c, *all_c[3:], *column_d, *parts_b])
    part_c, last_c, column_d, parts_b = tick[0], tick[1:3], tick[3 : 4 + len(far_masks)], tick[4 + len(far_masks) :]
    all_d = last_exchange(column_d)
    (made_c,) = project_pieces(last_c, part_c, 0, jnp.bfloat16)
    parts_c = sent_round(made_c)
    (part_d,) = project_pieces(all_d[:2], own_total, 3, jnp.float32)
    result = attend_head(1, tied(both_sides(parts_b), parts_c[0]), result)

    tick = tied([result, part_d, *all_d[2:]])
    result, part_d, last_d = tick[0], tick[1], tick[2:4]
    (made_d,) = project_pieces(last_d, part_d, 0, jnp.bfloat16)
    parts_d = sent_round(made_d)
    tick = tied([parts_d[0], *parts_c])
    parts_d[0], parts_c = tick[0], tick[1:]
    result = attend_head(2, tied(both_sides(parts_c), parts_d[0]), result)
    result, *parts_d = tied([result, *parts_d])
    result = attend_head(3, both_sides(parts_d), result)
    return result[None]


def solution(mesh):
    in_specs = (
        P("dp", "ctx", None),
        P("dp", "ctx", None),
        P("dp", None),
        P("dp"),
        P(("dp", "ctx"), None),
        P(("dp", "ctx"), None),
    )
    out_specs = P("dp", "ctx", None)
    return jax.shard_map(
        per_device, mesh=mesh, in_specs=in_specs, out_specs=out_specs, check_vma=False
    )
```

```python
import functools

import jax
import jax.numpy as jnp
from jax import lax
from jax.experimental import pallas as pl
from jax.experimental.pallas import tpu as pltpu
from jax.sharding import PartitionSpec as P

HEAD_WIDTH = 128
LOG2_E = 1.4426950408889634
ARRANGE_LIMIT = 12 * 2**20
PROJECT_LIMIT = 18 * 2**20
ATTEND_LIMIT = 14 * 2**20
REGROUP_LIMIT = 10 * 2**20


def swapped(value, mask):
    size = lax.axis_size("ctx")
    return lax.ppermute(value, "ctx", [(i, i ^ mask) for i in range(size)])


def across(value, mask):
    size = lax.axis_size("dp")
    return lax.ppermute(value, "dp", [(i, i ^ mask) for i in range(size)])


def arrange_kernel(blocks, starts, own_ref, other_ref, out_ref, sems):
    core = starts[0]
    rows = own_ref.shape[0]
    depth = own_ref.shape[1] // blocks
    copies = []
    for source, place in ((own_ref, core), (other_ref, 1 - core)):
        for index in range(blocks):
            first = pl.multiple_of(starts[1 + index] * depth, depth)
            copies.append(
                pltpu.make_async_copy(
                    source.at[:, pl.ds(first, depth)],
                    out_ref.at[pl.ds(pl.multiple_of(place * rows, rows), rows), pl.ds(index * depth, depth)],
                    sems.at[len(copies)],
                )
            )
    for copy in copies:
        copy.start()
    for copy in copies:
        copy.wait()


def arrange(starts, own, other):
    blocks = starts.shape[0] - 1
    rows, columns = own.shape
    anywhere = pl.BlockSpec(memory_space=pl.ANY)
    return pl.pallas_call(
        functools.partial(arrange_kernel, blocks),
        out_shape=jax.ShapeDtypeStruct((2 * rows, columns), own.dtype),
        in_specs=[pl.BlockSpec(memory_space=pltpu.SMEM), anywhere, anywhere],
        out_specs=pl.BlockSpec(memory_space=pltpu.VMEM),
        scratch_shapes=[pltpu.SemaphoreType.DMA((2 * blocks,))],
        compiler_params=pltpu.CompilerParams(vmem_limit_bytes=ARRANGE_LIMIT),
        cost_estimate=pl.CostEstimate(flops=0, bytes_accessed=8 * rows * columns, transcendentals=0),
        name="arrange",
    )(starts, own, other)


def project_kernel(runs, column, count, has_total, tokens, *refs):
    pieces, outs = refs[:count], refs[count + has_total :]
    width = sum(out.shape[1] for out in outs)
    total = refs[count][:, column : column + width] if has_total else None
    for piece, row, place, depth in runs:
        part = jnp.dot(
            tokens[:, place : place + depth], pieces[piece][row : row + depth, :], preferred_element_type=jnp.float32
        )
        total = part if total is None else total + part
    first = 0
    for out in outs:
        out[...] = total[:, first : first + out.shape[1]].astype(out.dtype)
        first += out.shape[1]


def project(tokens, runs, pieces, total, column, dtype, outs):
    rows, width = tokens.shape[0], pieces[0].shape[1]
    vmem = pl.BlockSpec(memory_space=pltpu.VMEM)
    depth = sum(run[3] for run in runs)
    totals = [] if total is None else [total]
    return pl.pallas_call(
        functools.partial(project_kernel, runs, column, len(pieces), len(totals)),
        out_shape=[jax.ShapeDtypeStruct((rows, width // outs), dtype)] * outs,
        in_specs=[vmem] * (1 + len(pieces) + len(totals)),
        out_specs=[vmem] * outs,
        compiler_params=pltpu.CompilerParams(vmem_limit_bytes=PROJECT_LIMIT),
        cost_estimate=pl.CostEstimate(flops=2 * rows * depth * width, bytes_accessed=2 * rows * depth, transcendentals=0),
        name="project",
    )(tokens, *pieces, *totals)


def attend_kernel(scale, group, query_first, side_first, short, flag, bias, queries, held, sent, *refs):
    out_ref, key_rows, value_rows, made, sems = refs[-5:]
    is_keys = flag[:1, :] > 0
    side = slice(side_first, side_first + HEAD_WIDTH)
    key_rows[...] = jnp.where(is_keys, held[:, side], sent[:, side])
    value_rows[:, :HEAD_WIDTH] = jnp.where(is_keys, sent[:, side], held[:, side])
    value_rows[:, HEAD_WIDTH:] = jnp.ones((value_rows.shape[0], HEAD_WIDTH), jnp.bfloat16)
    step = 128

    def unit(head, row):
        columns = slice(query_first + head * HEAD_WIDTH, query_first + (head + 1) * HEAD_WIDTH)
        span = pl.ds(row, step)
        scores = lax.dot_general(
            queries[span, columns], key_rows[...], (((1,), (1,)), ((), ())), preferred_element_type=jnp.float32
        )
        scores = scores * scale + bias[span, :]
        peak = jnp.max(scores, axis=1, keepdims=True)
        probs = jnp.exp2(scores - peak).astype(jnp.bfloat16)
        summed = jnp.dot(probs, value_rows[...], preferred_element_type=jnp.float32)
        made[head, span, :] = (summed[:, :HEAD_WIDTH] / summed[:, HEAD_WIDTH:]).astype(made.dtype)

    if short:
        @pl.loop(0, queries.shape[0] // step)
        def _(block):
            for head in range(group):
                unit(head, pl.multiple_of(block * step, step))

    copies = []
    for head in range(group):
        if not short:
            for row in range(0, queries.shape[0], step):
                unit(head, row)
        columns = slice(query_first + head * HEAD_WIDTH, query_first + (head + 1) * HEAD_WIDTH)
        copies.append(pltpu.make_async_copy(made.at[head], out_ref.at[:, columns], sems.at[head]))
        copies[-1].start()
    for copy in copies:
        copy.wait()


def attend(flag, bias, queries, sides, before, head, side_head, kv_heads):
    rows, width = queries.shape
    block = width // kv_heads
    group = block // HEAD_WIDTH
    count = bias.shape[1]
    vmem = pl.BlockSpec(memory_space=pltpu.VMEM)
    anywhere = pl.BlockSpec(memory_space=pl.ANY)
    operands = [flag, bias, queries, *sides]
    in_specs = [vmem] * 5
    aliases = {}
    if before is not None:
        aliases = {len(operands): 0}
        in_specs.append(anywhere)
        operands.append(before)
    return pl.pallas_call(
        functools.partial(attend_kernel, HEAD_WIDTH**-0.5 * LOG2_E, group, head * block, side_head * HEAD_WIDTH, before is None),
        out_shape=jax.ShapeDtypeStruct((rows, width), jnp.bfloat16),
        in_specs=in_specs,
        out_specs=anywhere,
        input_output_aliases=aliases,
        scratch_shapes=[
            pltpu.VMEM((count, HEAD_WIDTH), jnp.bfloat16),
            pltpu.VMEM((count, 2 * HEAD_WIDTH), jnp.bfloat16),
            pltpu.VMEM((group, rows, HEAD_WIDTH), jnp.bfloat16),
            pltpu.SemaphoreType.DMA((group,)),
        ],
        compiler_params=pltpu.CompilerParams(vmem_limit_bytes=ATTEND_LIMIT),
        cost_estimate=pl.CostEstimate(
            flops=4 * rows * block * count,
            bytes_accessed=8 * rows * block,
            transcendentals=rows * count * block // HEAD_WIDTH,
        ),
        name="attend",
    )(*operands)


def regroup_kernel(groups, count, *refs):
    for group, out_ref in zip(groups, refs[count:]):
        place = 0
        for index, row, rows, column in group:
            out_ref[place : place + rows, :] = refs[index][row : row + rows, column : column + out_ref.shape[1]]
            place += rows


def regroup(arrays, groups, widths):
    vmem = pl.BlockSpec(memory_space=pltpu.VMEM)
    return pl.pallas_call(
        functools.partial(regroup_kernel, groups, len(arrays)),
        out_shape=[
            jax.ShapeDtypeStruct((sum(part[2] for part in group), width), arrays[0].dtype)
            for group, width in zip(groups, widths)
        ],
        in_specs=[vmem] * len(arrays),
        out_specs=[vmem] * len(groups),
        compiler_params=pltpu.CompilerParams(vmem_limit_bytes=REGROUP_LIMIT),
        cost_estimate=pl.CostEstimate(flops=0, bytes_accessed=4 * sum(array.size for array in arrays), transcendentals=0),
        name="regroup",
    )(*arrays)


def assemble_kernel(flag, mine, theirs, out_ref):
    rows = mine.shape[0]
    is_first = flag[:1, :1] > 0
    out_ref[:rows, :] = jnp.where(is_first, mine[...], theirs[...])
    out_ref[rows:, :] = jnp.where(is_first, theirs[...], mine[...])


def assemble(flag, mine, theirs):
    rows, width = mine.shape
    vmem = pl.BlockSpec(memory_space=pltpu.VMEM)
    return pl.pallas_call(
        assemble_kernel,
        out_shape=jax.ShapeDtypeStruct((2 * rows, width), mine.dtype),
        in_specs=[vmem] * 3,
        out_specs=vmem,
        compiler_params=pltpu.CompilerParams(vmem_limit_bytes=REGROUP_LIMIT),
        name="assemble",
    )(flag, mine, theirs)


def per_device(hidden, queries, layout, boundary, key_matrix, value_matrix):
    tokens, order, start_doc = hidden[0], layout[0], boundary[0]
    rows_here = tokens.shape[0]
    half = rows_here // 2
    kv_width = key_matrix.shape[1]
    kv_heads = kv_width // HEAD_WIDTH
    ctx_count, dp_count = lax.axis_size("ctx"), lax.axis_size("dp")
    here, window = lax.axis_index("ctx"), lax.axis_index("dp")
    core = here % 2
    chips = ctx_count // 2
    masks = [1 << bit for bit in range(1, ctx_count.bit_length() - 1)]

    is_keys = core == 0
    mine = jnp.where(is_keys, key_matrix, value_matrix)
    theirs = swapped(jnp.where(is_keys, value_matrix, key_matrix), 1)
    flag = jnp.broadcast_to(is_keys.astype(jnp.float32), (8, HEAD_WIDTH))
    matrix = assemble(flag, mine, theirs)
    (other_tokens, _) = lax.optimization_barrier((tokens, theirs))
    other_tokens = swapped(other_tokens, 1)

    depth = matrix.shape[0] // 2
    far_masks = [1 << bit for bit in reversed(range(dp_count.bit_length() - 1))]

    def by_plane(piece, mask):
        return swapped(piece[0], mask), [(by, xor ^ mask, part) for by, xor, part in piece[1]]

    def by_column(piece, mask):
        return across(piece[0], mask), [(by ^ mask, xor, part) for by, xor, part in piece[1]]

    def view(piece, first_name=0, count=None, start=0, columns=None):
        array, names = piece
        names = names[first_name : None if count is None else first_name + count]
        return array, first_name * depth, names, start, array.shape[1] - start if columns is None else columns

    def first(piece, **columns):
        return view(piece, 0, len(piece[1]) // 2, **columns)

    def second(piece, **columns):
        return view(piece, len(piece[1]) // 2, **columns)

    def joined(*lists):
        arrays, groups = [], []
        for views in lists:
            group = []
            for array, row, names, start, _ in views:
                index = [k for k, known in enumerate(arrays) if known is array]
                if not index:
                    arrays.append(array)
                    index = [len(arrays) - 1]
                group.append((index[0], row, len(names) * depth, start))
            groups.append(tuple(group))
        made = regroup(arrays, tuple(groups), [views[0][4] for views in lists])
        return [(rows, sum([one[2] for one in views], [])) for rows, views in zip(made, lists)]

    def nearby(piece):
        for mask in masks[2:]:
            (piece,) = joined([view(piece), view(by_plane(piece, mask))])
        return [piece, by_plane(piece, masks[0]), by_plane(piece, masks[1])]

    def onward(pieces):
        low, high = joined([first(pieces[1])], [second(pieces[2])])
        return pieces + [by_plane(low, masks[1]), by_plane(high, masks[0])]

    def along(held, mask):
        whole = held[0] if len(held) == 1 else joined([view(piece) for piece in held])[0]
        return held + [by_column(whole, mask)]

    def tied(values, *others):
        arrays = [value[0] if isinstance(value, tuple) else value for value in values]
        after = lax.optimization_barrier((*arrays, *others))
        return [(array, value[1]) if isinstance(value, tuple) else array for array, value in zip(after, values)]

    plane = list(range(2, ctx_count, 2))

    def sent_round(made):
        return [made] + [swapped(made, xor) for xor in plane]

    def both_sides(parts):
        rows, width = parts[0].shape
        (held,) = regroup(parts, (tuple((index, 0, rows, 0) for index in range(len(parts))),), [width])
        return held, swapped(held, 1)

    sources = [(here // 2 * 2 ^ xor) + side for xor in [0] + plane for side in range(2)]
    block_ids = jnp.arange(order.shape[0], dtype=jnp.int32)

    def positions(devices):
        blocks = (jnp.stack(devices)[:, None] * 2 + jnp.arange(2)[None, :]).reshape(-1)
        looked = jnp.sum(jnp.where(blocks[:, None] == block_ids[None, :], order[None, :], 0), axis=1)
        return (looked[:, None] * half + jnp.arange(half, dtype=jnp.int32)[None, :]).reshape(-1)

    query_pos = positions([here])[:, None]
    key_pos = positions(sources)[None, :]
    allowed = (key_pos <= query_pos) & ((key_pos >= start_doc) | (query_pos < start_doc))
    bias = jnp.where(allowed, 0.0, -jnp.inf).astype(jnp.float32)

    cuts = [(0, 1), (1, 2), (3, 1)]

    def cut(index):
        start, count = cuts[index]
        return {"start": start * HEAD_WIDTH, "columns": count * HEAD_WIDTH}

    column = [0]
    for mask in far_masks:
        column = column + [by ^ mask for by in column]
    plane_xors = [0, masks[0], masks[1], masks[0] ^ masks[1]]
    for mask in masks[2:]:
        plane_xors = plane_xors + [xor ^ mask for xor in plane_xors]
    own_order = [(0, xor, part) for xor in plane_xors for part in range(2)]
    order_of = own_order + [(by, xor, part) for xor in plane_xors for part in range(2) for by in column[1:]]
    starts = [((window ^ by) * chips + ((here ^ xor) // 2)) * 2 + part for by, xor, part in order_of]
    ordered = depth % 128 == 0
    if ordered:
        arranged = arrange(jnp.stack([core, *starts]).astype(jnp.int32), tokens, other_tokens)
    else:
        both = jnp.where(is_keys, 0, 1)
        arranged = jnp.stack((tokens, other_tokens))[jnp.stack((both, 1 - both))].reshape(2 * rows_here, -1)
        arranged = jnp.take(arranged.reshape(2 * rows_here, -1, depth), jnp.stack(starts), axis=1)
        arranged = arranged.reshape(2 * rows_here, -1)

    def project_pieces(pieces, total, start, dtype):
        runs = []
        for index, (_, names) in enumerate(pieces):
            for block, name in enumerate(names):
                row, place = block * depth, order_of.index(name) * depth
                if runs and runs[-1][0] == index and runs[-1][2] + runs[-1][3] == place:
                    runs[-1] = (*runs[-1][:3], runs[-1][3] + depth)
                else:
                    runs.append((index, row, place, depth))
        return project(arranged, tuple(runs), [rows for rows, _ in pieces], total, start * HEAD_WIDTH, dtype, 1)

    def project_cut(index, pieces):
        return project_pieces(pieces, own_total, cuts[index][0], jnp.bfloat16)

    def attend_head(head, held, result, side_head=0):
        return attend(flag, bias, queries[0], held, result, head, side_head, kv_heads)

    mine_rows = (matrix, [(0, 0, 0), (0, 0, 1)])
    own = nearby(mine_rows)
    column_a = along(joined([view(mine_rows, **cut(0))]), far_masks[0])
    for mask in far_masks[1:]:
        column_a = along(column_a, mask)

    def halves(index):
        low = [first(own[0], **cut(index)), first(own[1], **cut(index))]
        high = [second(own[0], **cut(index)), second(own[2], **cut(index))]
        return low + high

    (start_b,) = tied(joined([view(mine_rows, **cut(1))]), column_a[-1][0])
    column_b = along([start_b], far_masks[0])
    all_own = onward(own)

    def sorted_views(held, places, **columns):
        size = len(held[0][1])
        part = size // places
        views = [[] for _ in range(places)]
        for piece in held[1:]:
            for block in range(0, len(piece[1]), size):
                for place in range(places):
                    views[place].append(view(piece, block + place * part, part, **columns))
        return views

    (rest_a,) = joined(sum(sorted_views(column_a, 2), []))
    near_a = nearby(rest_a)

    def last_exchange(held):
        views = sorted_views(held, 4)
        low, high = joined(views[0] + views[1], views[2] + views[3])
        return [low, high, by_plane(low, masks[1]), by_plane(high, masks[0])]

    tick = tied([arranged, *near_a, *all_own, *column_b])
    arranged, near_a, all_own, column_b = tick[0], tick[1:4], tick[4:9], tick[9:]
    all_a = onward(near_a)
    for mask in far_masks[1:]:
        column_b = along(column_b, mask)
    (own_total,) = project_pieces(all_own, None, 0, jnp.float32)

    tick = tied([own_total, *all_a])
    own_total, all_a = tick[0], tick[1:]
    (made_a,) = project_cut(0, all_a)
    parts_a = sent_round(made_a)
    rest_b, rest_c = joined(
        *[sum(sorted_views(column_b, 2, start=first * HEAD_WIDTH, columns=HEAD_WIDTH), []) for first in range(2)]
    )
    near_b = nearby(rest_b)
    (made_a,) = project_cut(0, all_a)
    parts_a = sent_round(made_a)
    (start_d, rest_c, *parts_a) = tied([*joined(halves(2)), rest_c, *parts_a])
    near_c = nearby(rest_c)
    column_d = along([start_d], far_masks[0])
    result = attend_head(0, both_sides(parts_a), None)

    tick = tied([result, *near_b])
    result, near_b = tick[0], tick[1:]
    all_b = onward(near_b)
    (part_b,) = project_pieces(all_b[:3], own_total, 1, jnp.float32)
    part_b, *column_d = tied([part_b, *column_d])
    for mask in far_masks[1:]:
        column_d = along(column_d, mask)

    tick = tied([part_b, *all_b[3:], *near_c])
    part_b, last_b, near_c = tick[0], tick[1:3], tick[3:]
    all_c = onward(near_c)
    (made_b,) = project_pieces(last_b, part_b, 0, jnp.bfloat16)
    parts_b = sent_round(made_b)
    (part_c,) = project_pieces(all_c[:3], own_total, 2, jnp.float32)

    tick = tied([part_c, *all_c[3:], *column_d, *parts_b])
    part_c, last_c, column_d, parts_b = tick[0], tick[1:3], tick[3 : 4 + len(far_masks)], tick[4 + len(far_masks) :]
    all_d = last_exchange(column_d)
    (made_c,) = project_pieces(last_c, part_c, 0, jnp.bfloat16)
    parts_c = sent_round(made_c)
    (part_d,) = project_pieces(all_d[:2], own_total, 3, jnp.float32)
    result = attend_head(1, tied(both_sides(parts_b), parts_c[0]), result)

    tick = tied([result, part_d, *all_d[2:]])
    result, part_d, last_d = tick[0], tick[1], tick[2:4]
    (made_d,) = project_pieces(last_d, part_d, 0, jnp.bfloat16)
    parts_d = sent_round(made_d)
    tick = tied([parts_d[0], *parts_c])
    parts_d[0], parts_c = tick[0], tick[1:]
    result = attend_head(2, tied(both_sides(parts_c), parts_d[0]), result)
    result, *parts_d = tied([result, *parts_d])
    result = attend_head(3, both_sides(parts_d), result)
    return result[None]


def solution(mesh):
    in_specs = (
        P("dp", "ctx", None),
        P("dp", "ctx", None),
        P("dp", None),
        P("dp"),
        P(("dp", "ctx"), None),
        P(("dp", "ctx"), None),
    )
    out_specs = P("dp", "ctx", None)
    return jax.shard_map(
        per_device, mesh=mesh, in_specs=in_specs, out_specs=out_specs, check_vma=False
    )
```
